1024 devices in a mesh: seq: 128 (over z, y), head: 8 (over x, core).
Axes of the slice: x: 4, y: 4, z: 32, core: 2. Of those that a mesh axis runs over, the one named last changes fastest.
Arguments:
- queries: bfloat16 [16384, 4096], P('seq', 'head'), may hold values from -40 to 40
- keys_in: bfloat16 [16384, 1024], P('seq', 'head'), may hold values from -4 to 4
- values_in: bfloat16 [16384, 1024], P('seq', 'head'), may hold values from -20 to 20
- norm_gain: float32 [4096], P('head'), may hold values from 0.1 to 1.9
- grad_out: bfloat16 [16384, 4096], P('seq', 'head'), may hold values from -6 to 6
- nearby_block_mask: int32 [128, 16], P('seq'), may hold values from 0 to 1, as said below
Outputs:
- normed_out: bfloat16 [16384, 4096], P('seq', 'head')
- grad_queries: bfloat16 [16384, 4096], P('seq', 'head')
- grad_keys: bfloat16 [16384, 1024], P('seq', 'head')
- grad_values: bfloat16 [16384, 1024], P('seq', 'head')
The draws below stay inside these ranges and needn't reach their ends.
Inputs may be any that keep to these rules, and one draw needn't show every extreme that they name: nearby_block_mask[b, j] is 0 wherever key block (b - 8) + j lies outside the scene, and 1 where that block is b itself.
All inputs are finite; a program needn't handle non-finite values.
Results may differ from the reference program's by a relative error of at most 0.013.
Values may be sent and summed in bfloat16 or wider, within the bound.
No kernel may reach another device: no remote copies, remote signals or barrier semaphores. Data moves between devices by JAX's collectives and lax.ppermute only.
A program may use at most 32 MiB of HBM per device.

```python
import jax
import jax.numpy as jnp
from jax import lax

HEADS = 32
KV_HEADS = 8
DH = 128
BLK = 128
TOK_DEV = 128
GROUP = 4
NEIGH = 16
QUERY_BLOCKS_SEQ = 1
TOKENS = 16384
SCENE_BLOCKS = 128
KEY_BLOCK_SLOTS = 16
FEAT = 4096
N_SEQ = 128


def draw_pair(key):
    base = jax.random.fold_in(key, 7)
    k_seed = jax.random.fold_in(base, 1)
    q_seed = jax.random.fold_in(base, 2)
    keys_all = jnp.clip(jax.random.normal(k_seed, (TOKENS, KV_HEADS, DH), jnp.float32), -4.0, 4.0)
    query_all = jnp.clip(jax.random.normal(q_seed, (TOKENS, KV_HEADS, GROUP, DH), jnp.float32), -4.0, 4.0)
    return (query_all.reshape(TOKENS, HEADS * DH), keys_all.reshape(TOKENS, KV_HEADS * DH))


def draw_queries(key, part):
    return draw_pair(key)[0].astype(jnp.bfloat16)


def draw_keys_in(key, part):
    return draw_pair(key)[1].astype(jnp.bfloat16)


def draw_values_in(key, part):
    column = jnp.arange(KV_HEADS * DH, dtype=jnp.int32) // DH
    head_factor = 1.0 + 2.0 * column.astype(jnp.float32) / max(KV_HEADS - 1, 1)
    spread = jnp.exp(jax.random.uniform(jax.random.fold_in(key, 21), (KV_HEADS * DH,), jnp.float32, 0.0, jnp.log(3.3)))
    source = jnp.clip(jax.random.normal(jax.random.fold_in(key, 23), (TOKENS, KV_HEADS * DH), jnp.float32), -4.0, 4.0)
    return (0.5 * source * head_factor * spread).astype(jnp.bfloat16)


def draw_nearby_block_mask(key, part):
    rows = jnp.arange(SCENE_BLOCKS, dtype=jnp.int32)[:, None]
    slot_positions = jnp.arange(KEY_BLOCK_SLOTS, dtype=jnp.int32)[None, :]
    device = rows // QUERY_BLOCKS_SEQ
    target = (device - NEIGH // 2) * QUERY_BLOCKS_SEQ + slot_positions
    inside = (target >= 0) & (target < SCENE_BLOCKS)
    level = jax.random.randint(jax.random.fold_in(key, 1), (SCENE_BLOCKS, 1), 1, 9)
    selected_blocks = jax.random.randint(jax.random.fold_in(key, 2), (SCENE_BLOCKS, KEY_BLOCK_SLOTS), 0, 64)
    listed = (selected_blocks < level * level) & inside
    itself = target == rows
    return jnp.where(itself | listed, 1, 0).astype(jnp.int32)


def block_scale(rng, shape, cuts, least, top_value):
    def one(position, parts):
        steps = jax.random.uniform(jax.random.fold_in(jax.random.fold_in(rng, 6), position), (parts,), jnp.float32, least / len(cuts), top_value / len(cuts))
        return jnp.repeat(jnp.exp(steps), shape[position] // parts).reshape((-1,) + (1,) * (len(shape) - position - 1))

    gain = one(*cuts[0])
    for cut in cuts[1:]:
        gain = gain * one(*cut)
    return gain


def scatter_about(stream_key, extent, width, limit, split=(), kind=jnp.bfloat16):
    entries = jax.random.normal(stream_key, extent, jnp.float32) * width
    if len(split) > 0:
        entries = block_scale(stream_key, extent, split, -0.22, 0.18) * entries
    return jnp.clip(entries, min=-limit, max=limit).astype(kind)


def setup_inputs(seed: int = 0) -> dict:
    key_of = jax.random.split(jax.random.key(seed), 7)
    queries = draw_queries(jax.random.fold_in(key_of[6], 71), 0)
    keys_in = draw_keys_in(jax.random.fold_in(key_of[6], 71), 0)
    values_in = draw_values_in(jax.random.fold_in(key_of[6], 71), 0)
    norm_gain = jnp.clip(1.0 + 0.18 * jax.random.normal(key_of[3], (FEAT,), jnp.float32), 0.1, 1.9)
    grad_out = scatter_about(key_of[4], (TOKENS, FEAT), 1.0, 6.0, ((0, 128), (1, 8)))
    nearby_block_mask = draw_nearby_block_mask(jax.random.fold_in(key_of[6], 71), 0)
    return dict(queries=queries, keys_in=keys_in, values_in=values_in, norm_gain=norm_gain, grad_out=grad_out, nearby_block_mask=nearby_block_mask)


NEGATIVE = -1e+30
EPSILON = 1e-06

def round_trip(values):
    return lax.optimization_barrier(values.astype(jnp.bfloat16)).astype(jnp.float32)

def token_mask(blocks):
    widened = jnp.repeat(jnp.repeat(blocks, BLK, axis=0), BLK, axis=1)
    return widened > 0

def block_scores(q_dev, k_dev, blocks):
    raw = jnp.einsum('qcge,tce->cgqt', q_dev.astype(jnp.float32), k_dev.astype(jnp.float32))
    raw = raw * DH ** (-0.5)
    return jnp.where(token_mask(blocks)[None, None], raw, NEGATIVE)

def pair_terms(q_dev, do_dev, lse_dev, delta_dev, k_dev, v_dev, blocks):
    scores = block_scores(q_dev, k_dev, blocks)
    prob = jnp.exp(scores - lse_dev[..., None])
    d_prob = jnp.einsum('qcge,tce->cgqt', do_dev.astype(jnp.float32), v_dev.astype(jnp.float32))
    d_score = round_trip(prob * (d_prob - delta_dev[..., None]))
    scaling = DH ** (-0.5)
    grad_q = round_trip(jnp.einsum('cgqt,tce->qcge', d_score, k_dev.astype(jnp.float32)) * scaling)
    grad_k = round_trip(jnp.einsum('cgqt,qcge->tce', d_score, q_dev.astype(jnp.float32)) * scaling)
    grad_v = round_trip(jnp.einsum('cgqt,qcge->tce', round_trip(prob), do_dev.astype(jnp.float32)))
    return (grad_q, grad_k, grad_v)

def reference(queries, keys_in, values_in, norm_gain, grad_out, nearby_block_mask):
    half_span = NEIGH // 2
    q_all = queries.reshape(N_SEQ, TOK_DEV, KV_HEADS, GROUP, DH)
    k_all = keys_in.reshape(N_SEQ, TOK_DEV, KV_HEADS, DH)
    v_all = values_in.reshape(N_SEQ, TOK_DEV, KV_HEADS, DH)
    gathered_mask = nearby_block_mask.reshape(N_SEQ, QUERY_BLOCKS_SEQ, KEY_BLOCK_SLOTS)

    def padded(array):
        return jnp.pad(array, ((half_span, half_span),) + ((0, 0),) * (array.ndim - 1))
    k_pad = padded(k_all)
    v_pad = padded(v_all)
    devices = jnp.arange(N_SEQ, dtype=jnp.int32)
    first = jnp.int32(0)
    last = jnp.int32(NEIGH)

    def forward_device(device):
        q_dev = q_all[device]
        rows_mask = gathered_mask[device]

        def blocks_of(slot):
            return lax.dynamic_slice_in_dim(rows_mask, slot * QUERY_BLOCKS_SEQ, QUERY_BLOCKS_SEQ, axis=1)

        def top_step(slot, row_top):
            blocks = blocks_of(slot)

            def update(current):
                return jnp.maximum(current, block_scores(q_dev, k_pad[device + slot], blocks).max(axis=-1))
            return lax.cond(jnp.any(blocks > 0), update, lambda current: current, row_top)
        row_top = lax.fori_loop(first, last, top_step, jnp.full((KV_HEADS, GROUP, TOK_DEV), NEGATIVE, jnp.float32))

        def sum_step(slot, carried):
            blocks = blocks_of(slot)

            def add_block(pair):
                row_total, numerator = pair
                scores = block_scores(q_dev, k_pad[device + slot], blocks)
                weights = jnp.exp(scores - row_top[..., None])
                part_sum = jnp.einsum('cgqt,tce->qcge', round_trip(weights), v_pad[device + slot].astype(jnp.float32))
                return (row_total + weights.sum(axis=-1), numerator + part_sum)
            return lax.cond(jnp.any(blocks > 0), add_block, lambda pair: pair, carried)
        start = (jnp.zeros((KV_HEADS, GROUP, TOK_DEV), jnp.float32), jnp.zeros((TOK_DEV, KV_HEADS, GROUP, DH), jnp.float32))
        row_total, numerator = lax.fori_loop(first, last, sum_step, start)
        attended = numerator / jnp.transpose(row_total, (2, 0, 1))[..., None]
        return (attended, row_top + jnp.log(row_total))
    attended_all, lse_all = lax.map(forward_device, devices)
    flat = attended_all.reshape(TOKENS, HEADS * DH)
    root = jnp.sqrt(lax.optimization_barrier(jnp.mean(flat * flat, axis=-1)) + EPSILON)
    normed = flat / root[:, None]
    normed_out = (norm_gain * normed).astype(jnp.bfloat16)
    upstream = grad_out.astype(jnp.float32) * norm_gain
    inner = lax.optimization_barrier(jnp.sum(upstream * normed, axis=-1))
    d_attended = ((upstream - normed * (inner / (HEADS * DH))[:, None]) / root[:, None]).astype(jnp.bfloat16)
    do_all = d_attended.reshape(N_SEQ, TOK_DEV, KV_HEADS, GROUP, DH)
    delta_all = jnp.transpose(lax.optimization_barrier(jnp.sum(do_all.astype(jnp.float32) * attended_all, axis=-1)), (0, 2, 3, 1))

    def query_device(device):
        q_dev = q_all[device]
        do_dev = do_all[device]
        lse_dev = lse_all[device]
        delta_dev = delta_all[device]
        rows_mask = gathered_mask[device]

        def step(slot, total):
            blocks = lax.dynamic_slice_in_dim(rows_mask, slot * QUERY_BLOCKS_SEQ, QUERY_BLOCKS_SEQ, axis=1)

            def add(current):
                terms = pair_terms(q_dev, do_dev, lse_dev, delta_dev, k_pad[device + slot], v_pad[device + slot], blocks)
                return current + terms[0]
            return lax.cond(jnp.any(blocks > 0), add, lambda current: current, total)
        return lax.fori_loop(first, last, step, jnp.zeros((TOK_DEV, KV_HEADS, GROUP, DH), jnp.float32))
    grad_q_all = lax.map(query_device, devices)
    q_pad = padded(q_all)
    do_pad = padded(do_all)
    lse_pad = padded(lse_all)
    delta_pad = padded(delta_all)
    mask_pad = padded(gathered_mask)

    def key_device(device):
        k_dev = k_all[device]
        v_dev = v_all[device]

        def step(slot, totals):
            source = device + NEIGH - slot
            blocks = lax.dynamic_slice_in_dim(mask_pad[source], slot * QUERY_BLOCKS_SEQ, QUERY_BLOCKS_SEQ, axis=1)

            def add(current):
                terms = pair_terms(q_pad[source], do_pad[source], lse_pad[source], delta_pad[source], k_dev, v_dev, blocks)
                return (current[0] + terms[1], current[1] + terms[2])
            return lax.cond(jnp.any(blocks > 0), add, lambda current: current, totals)
        start = (jnp.zeros((TOK_DEV, KV_HEADS, DH), jnp.float32), jnp.zeros((TOK_DEV, KV_HEADS, DH), jnp.float32))
        return lax.fori_loop(first, last, step, start)
    grad_k_all, grad_v_all = lax.map(key_device, devices)
    grad_queries = grad_q_all.reshape(TOKENS, HEADS * DH).astype(jnp.bfloat16)
    grad_keys = grad_k_all.reshape(TOKENS, KV_HEADS * DH).astype(jnp.bfloat16)
    grad_values = grad_v_all.reshape(TOKENS, KV_HEADS * DH).astype(jnp.bfloat16)
    return (normed_out, grad_queries, grad_keys, grad_values)
```

```python
import math

import jax
import jax.numpy as jnp
from jax import lax
from jax.experimental import pallas as pl
from jax.experimental.pallas import tpu as pltpu
from jax.sharding import Mesh
from jax.sharding import PartitionSpec as P

HEADS = 32
KV_HEADS = 8
GROUP = HEADS // KV_HEADS
DH = 128
BLK = 128
ROWS = GROUP * BLK
SLOTS = 16
CHUNK = 256
NEGATIVE = -1e30
EPSILON = 1e-06
FEATURES = HEADS * DH
SCALING = DH ** (-0.5)
EXP2_SCALE = SCALING / math.log(2.0)
PAIR = ("zp", "y")
VMEM_LIMIT = 40 * 1024 * 1024


def window_slot(zp, y, peer, part):
    peer_zp, peer_y = peer // 4, peer % 4
    across = (zp - peer_zp) & 1
    shift = peer_y - y
    if part == 0:
        return 8 + shift + across * (4 * (1 - 2 * zp))
    same = shift & 15
    other = 8 + shift - 4 * (1 - 2 * zp)
    return jnp.where(across == 1, other, same)


def stacked(array):
    return jnp.concatenate([array[:, g * DH : (g + 1) * DH] for g in range(GROUP)], axis=0)


def stacked_t(array):
    return jnp.concatenate([array[:, g * DH : (g + 1) * DH].T for g in range(GROUP)], axis=1)


def unstacked_t(array):
    return jnp.concatenate([array[:, g * BLK : (g + 1) * BLK].T for g in range(GROUP)], axis=1)


def over_groups(row):
    return sum(row[:, g * BLK : (g + 1) * BLK] for g in range(GROUP))


def to_groups(row):
    return jnp.concatenate([row] * GROUP, axis=1)


def forward_kernel(place, mask, q_ref, kv_ref, up_ref, gain_ref, w_ref, att_ref, up_out, inv_ref, part_ref, s_ref):
    zp, y = place[0], place[1]
    q_t = stacked_t(q_ref[...])
    top = jnp.full((8, ROWS), NEGATIVE, jnp.float32)
    for slot in range(SLOTS):
        rows = pl.ds(slot * BLK, BLK)
        column = window_slot(zp, y, slot // 2, slot % 2)
        bias = jnp.where(mask[0, column] > 0, 0.0, NEGATIVE)
        raw = jnp.dot(kv_ref[rows, :DH], q_t, preferred_element_type=jnp.float32) + bias
        s_ref[rows, :] = raw
        top = jnp.maximum(top, raw.reshape(BLK // 8, 8, ROWS).max(axis=0))
    top = top.max(axis=0, keepdims=True)
    total = jnp.zeros((8, ROWS), jnp.float32)
    numer = jnp.zeros((DH, ROWS), jnp.float32)
    for chunk in range(SLOTS * BLK // CHUNK):
        rows = pl.ds(chunk * CHUNK, CHUNK)
        weights = jnp.exp2((s_ref[rows, :] - top) * EXP2_SCALE)
        total = total + weights.reshape(CHUNK // 8, 8, ROWS).sum(axis=0)
        rounded = weights.astype(jnp.bfloat16)
        w_ref[rows, :] = rounded
        numer = numer + jnp.dot(kv_ref[rows, DH:].T, rounded, preferred_element_type=jnp.float32)
    inverse = 1.0 / total.sum(axis=0, keepdims=True)
    attended = numer * inverse
    att_ref[...] = attended
    inv_ref[...] = jnp.broadcast_to(inverse, (8, ROWS))
    upstream = stacked_t(up_ref[...].astype(jnp.float32) * gain_ref[...])
    up_out[...] = upstream
    squares = over_groups(jnp.sum(attended * attended, axis=0, keepdims=True))
    products = over_groups(jnp.sum(upstream * attended, axis=0, keepdims=True))
    part_ref[...] = jnp.concatenate([squares, products], axis=0)


def backward_kernel(q_ref, kv_ref, w_ref, att_ref, up_ref, inv_ref, sums_ref, gain_ref, terms_ref, ds_ref, out_ref):
    sums = sums_ref[0]
    for peer in range(1, KV_HEADS):
        sums = sums + sums_ref[peer]
    root = jnp.sqrt(sums[0:1] / FEATURES + EPSILON)
    inv_root = 1.0 / root
    inner = sums[1:2] * inv_root
    attended = att_ref[...]
    normed = attended * to_groups(inv_root)
    out_ref[...] = (unstacked_t(normed) * gain_ref[...]).astype(jnp.bfloat16)
    d_att = (up_ref[...] - normed * to_groups(inner / FEATURES)) * to_groups(inv_root)
    d_att = d_att.astype(jnp.bfloat16).astype(jnp.float32)
    inverse = inv_ref[0:1]
    delta = jnp.sum(d_att * attended, axis=0, keepdims=True) * inverse
    do_t = (d_att * inverse).astype(jnp.bfloat16)
    do_rows = jnp.concatenate([do_t[:, g * BLK : (g + 1) * BLK].T for g in range(GROUP)], axis=0)
    q_rows = stacked(q_ref[...])
    for chunk in range(SLOTS * BLK // CHUNK):
        rows = pl.ds(chunk * CHUNK, CHUNK)
        weights = w_ref[rows, :]
        d_prob = jnp.dot(kv_ref[rows, DH:], do_t, preferred_element_type=jnp.float32)
        d_score = (weights.astype(jnp.float32) * (d_prob - delta)).astype(jnp.bfloat16)
        ds_ref[rows, :] = d_score
        term_k = jnp.dot(d_score, q_rows, preferred_element_type=jnp.float32) * SCALING
        term_v = jnp.dot(weights, do_rows, preferred_element_type=jnp.float32)
        terms_ref[rows, :DH] = term_k.astype(jnp.bfloat16)
        terms_ref[rows, DH:] = term_v.astype(jnp.bfloat16)


def query_kernel(kv_ref, ds_ref, grad_ref):
    grad = jnp.zeros((DH, ROWS), jnp.float32)
    for chunk in range(SLOTS * BLK // CHUNK):
        rows = pl.ds(chunk * CHUNK, CHUNK)
        grad = grad + jnp.dot(kv_ref[rows, :DH].T, ds_ref[rows, :], preferred_element_type=jnp.float32)
    grad_ref[...] = (unstacked_t(grad) * SCALING).astype(jnp.bfloat16)


def shape(dims, dtype):
    return jax.ShapeDtypeStruct(dims, dtype)


def in_vmem(count):
    return [pl.BlockSpec(memory_space=pltpu.VMEM)] * count


def in_smem(count):
    return [pl.BlockSpec(memory_space=pltpu.SMEM)] * count


def two_planes(array, by):
    length = lax.axis_size("zq")
    return lax.ppermute(array, "zq", [(i, (i + by) % length) for i in range(length)])


def per_device(queries, keys_in, values_in, norm_gain, grad_out, nearby_block_mask):
    zp, y = lax.axis_index("zp"), lax.axis_index("y")
    place = jnp.stack([zp, y]).astype(jnp.int32)
    gain = norm_gain.reshape(1, -1)
    own = jnp.concatenate([keys_in, values_in], axis=1)
    above = two_planes(own, -1)
    below = two_planes(own, 1)
    to_zp = jnp.arange(8, dtype=jnp.int32)[:, None, None] // 4
    to_y = jnp.arange(8, dtype=jnp.int32)[:, None, None] % 4
    take_below = jnp.where(to_zp == zp, y >= to_y, zp == 1)
    second = jnp.where(take_below, below[None], above[None])
    sent = jnp.stack([jnp.broadcast_to(own[None], second.shape), second], axis=1)
    gathered = lax.all_to_all(sent, PAIR, 0, 0).reshape(SLOTS * BLK, 2 * DH)

    weights, attended, upstream, inverse, part = pl.pallas_call(
        forward_kernel,
        out_shape=(
            shape((SLOTS * BLK, ROWS), jnp.bfloat16),
            shape((DH, ROWS), jnp.float32),
            shape((DH, ROWS), jnp.float32),
            shape((8, ROWS), jnp.float32),
            shape((2, BLK), jnp.float32),
        ),
        in_specs=in_smem(2) + in_vmem(4),
        out_specs=tuple(in_vmem(5)),
        scratch_shapes=[pltpu.VMEM((SLOTS * BLK, ROWS), jnp.float32)],
        compiler_params=pltpu.CompilerParams(vmem_limit_bytes=VMEM_LIMIT),
        cost_estimate=pl.CostEstimate(flops=540_000_000, bytes_accessed=4_000_000, transcendentals=1_050_000),
        name="forward",
    )(place, nearby_block_mask, queries, gathered, grad_out, gain)
    sums = lax.all_to_all(jnp.broadcast_to(part[None], (KV_HEADS, 2, BLK)), "head", 0, 0)
    terms, d_score, normed_out = pl.pallas_call(
        backward_kernel,
        out_shape=(
            shape((SLOTS * BLK, 2 * DH), jnp.bfloat16),
            shape((SLOTS * BLK, ROWS), jnp.bfloat16),
            shape((BLK, GROUP * DH), jnp.bfloat16),
        ),
        in_specs=in_vmem(8),
        out_specs=tuple(in_vmem(3)),
        compiler_params=pltpu.CompilerParams(vmem_limit_bytes=VMEM_LIMIT),
        cost_estimate=pl.CostEstimate(flops=810_000_000, bytes_accessed=6_000_000, transcendentals=0),
        name="backward",
    )(queries, gathered, weights, attended, upstream, inverse, sums, gain)
    returned = lax.all_to_all(terms.reshape(8, 2, BLK, 2 * DH), PAIR, 0, 0)
    grad_queries = pl.pallas_call(
        query_kernel,
        out_shape=shape((BLK, GROUP * DH), jnp.bfloat16),
        in_specs=in_vmem(2),
        out_specs=in_vmem(1)[0],
        compiler_params=pltpu.CompilerParams(vmem_limit_bytes=VMEM_LIMIT),
        cost_estimate=pl.CostEstimate(flops=270_000_000, bytes_accessed=3_200_000, transcendentals=0),
        name="query_grad",
    )(gathered, d_score)
    wide = returned.astype(jnp.float32)
    own_sum = wide[:, 0].sum(axis=0)
    is_below = take_below
    to_below = jnp.where(is_below, wide[:, 1], 0.0).sum(axis=0).astype(jnp.bfloat16)
    to_above = jnp.where(is_below, 0.0, wide[:, 1]).sum(axis=0).astype(jnp.bfloat16)
    from_above = two_planes(to_below, -1)
    from_below = two_planes(to_above, 1)
    total = own_sum + from_above.astype(jnp.float32) + from_below.astype(jnp.float32)
    total = total.astype(jnp.bfloat16)
    return normed_out, grad_queries, total[:, :DH], total[:, DH:]


def solution(mesh):
    spans, heads = mesh.devices.shape
    fine = Mesh(mesh.devices.reshape(spans // 8, 2, 4, heads), ("zq", "zp", "y", "head"))
    seq = ("zq", "zp", "y")
    both = P(seq, "head")
    return jax.shard_map(
        per_device,
        mesh=fine,
        in_specs=(both, both, both, P("head"), both, P(seq, None)),
        out_specs=(both, both, both, both),
        check_vma=False,
    )
```

```python
import math

import jax
import jax.numpy as jnp
from jax import lax
from jax.experimental import pallas as pl
from jax.experimental.pallas import tpu as pltpu
from jax.sharding import Mesh
from jax.sharding import PartitionSpec as P

HEADS = 32
KV_HEADS = 8
GROUP = HEADS // KV_HEADS
DH = 128
BLK = 128
ROWS = GROUP * BLK
PEERS = 8
NEGATIVE = -1e30
EPSILON = 1e-06
FEATURES = HEADS * DH
SCALING = DH ** (-0.5)
EXP2_SCALE = SCALING / math.log(2.0)
PAIR = ("zp", "y")
VMEM_LIMIT = 12 * 1024 * 1024


def window_slot(zp, y, peer, part):
    peer_zp, peer_y = peer // 4, peer % 4
    across = (zp - peer_zp) & 1
    shift = peer_y - y
    if part == 0:
        return 8 + shift + across * (4 * (1 - 2 * zp))
    same = shift & 15
    other = 8 + shift - 4 * (1 - 2 * zp)
    return jnp.where(across == 1, other, same)


def stacked(array):
    return jnp.concatenate([array[:, g * DH : (g + 1) * DH] for g in range(GROUP)], axis=0)


def stacked_t(array):
    return jnp.concatenate([array[:, g * DH : (g + 1) * DH].T for g in range(GROUP)], axis=1)


def unstacked_t(array):
    return jnp.concatenate([array[:, g * BLK : (g + 1) * BLK].T for g in range(GROUP)], axis=1)


def over_groups(row):
    return sum(row[:, g * BLK : (g + 1) * BLK] for g in range(GROUP))


def to_groups(row):
    return jnp.concatenate([row] * GROUP, axis=1)


def forward_half(part, place, mask, q_t, kv_ref, w_ref, s_ref):
    zp, y = place[0], place[1]
    top = jnp.full((8, ROWS), NEGATIVE, jnp.float32)
    for peer in range(PEERS):
        bias = jnp.where(mask[0, window_slot(zp, y, peer, part)] > 0, 0.0, NEGATIVE)
        raw = jnp.dot(kv_ref[peer, 0], q_t, preferred_element_type=jnp.float32) + bias
        s_ref[peer] = raw
        top = jnp.maximum(top, raw.reshape(BLK // 8, 8, ROWS).max(axis=0))
    top = top.max(axis=0, keepdims=True)
    total = jnp.zeros((8, ROWS), jnp.float32)
    numer = jnp.zeros((DH, ROWS), jnp.float32)
    for peer in range(PEERS):
        weights = jnp.exp2((s_ref[peer] - top) * EXP2_SCALE)
        total = total + weights.reshape(BLK // 8, 8, ROWS).sum(axis=0)
        rounded = weights.astype(jnp.bfloat16)
        w_ref[peer] = rounded
        numer = numer + jnp.dot(kv_ref[peer, 1].T, rounded, preferred_element_type=jnp.float32)
    return top, total.sum(axis=0, keepdims=True), numer


def near_kernel(place, mask, q_ref, kv_ref, up_ref, gain_ref, w_ref, num_ref, up_out, stat_ref, s_ref):
    q_t = stacked_t(q_ref[...])
    top, total, numer = forward_half(0, place, mask, q_t, kv_ref, w_ref, s_ref)
    num_ref[...] = numer
    stat_ref[...] = jnp.concatenate([top, total] * 4, axis=0)
    up_out[...] = stacked_t(up_ref[...].astype(jnp.float32) * gain_ref[...])


def far_kernel(place, mask, q_ref, kv_ref, num_ref, up_ref, stat_ref, w_ref, att_ref, inv_ref, part_ref, s_ref):
    q_t = stacked_t(q_ref[...])
    top, total, numer = forward_half(1, place, mask, q_t, kv_ref, w_ref, s_ref)
    near_top, near_total = stat_ref[0:1], stat_ref[1:2]
    both = jnp.maximum(top, near_top)
    far_scale = jnp.exp2((top - both) * EXP2_SCALE)
    near_scale = jnp.exp2((near_top - both) * EXP2_SCALE)
    inverse = 1.0 / (total * far_scale + near_total * near_scale)
    far_scale, near_scale = far_scale * inverse, near_scale * inverse
    attended = numer * far_scale + num_ref[...] * near_scale
    att_ref[...] = attended
    inv_ref[...] = jnp.concatenate([near_scale, far_scale] * 4, axis=0)
    squares = over_groups(jnp.sum(attended * attended, axis=0, keepdims=True))
    products = over_groups(jnp.sum(up_ref[...] * attended, axis=0, keepdims=True))
    part_ref[...] = jnp.concatenate([squares, products], axis=0)


def scaled_upstream(d_att, delta, inverse):
    delta = delta * inverse
    do_t = (d_att * inverse).astype(jnp.bfloat16)
    return do_t, delta


def score_grad(values, weights, do_t, delta):
    d_prob = jnp.dot(values, do_t, preferred_element_type=jnp.float32)
    return (weights.astype(jnp.float32) * (d_prob - delta)).astype(jnp.bfloat16)


def send_terms(peer, weights, d_score, do_rows, q_rows, terms_ref, held, sent):
    term_k = jnp.dot(d_score, q_rows, preferred_element_type=jnp.float32) * SCALING
    term_v = jnp.dot(weights, do_rows, preferred_element_type=jnp.float32)
    held[peer, 0] = term_k.astype(jnp.bfloat16)
    held[peer, 1] = term_v.astype(jnp.bfloat16)
    copy = pltpu.make_async_copy(held.at[peer], terms_ref.at[peer], sent.at[peer])
    copy.start()
    return copy


def rows_of(do_t):
    return jnp.concatenate([do_t[:, g * BLK : (g + 1) * BLK].T for g in range(GROUP)], axis=0)


def far_back_kernel(q_ref, kv_ref, w_ref, att_ref, up_ref, inv_ref, sums_ref, terms_ref, do_ref, delta_ref, root_ref, held, sent):
    sums = sums_ref[0]
    for peer in range(1, KV_HEADS):
        sums = sums + sums_ref[peer]
    root = jnp.sqrt(sums[0:1] / FEATURES + EPSILON)
    inv_root = 1.0 / root
    inner = sums[1:2] * inv_root
    attended = att_ref[...]
    normed = attended * to_groups(inv_root)
    d_att = (up_ref[...] - normed * to_groups(inner / FEATURES)) * to_groups(inv_root)
    d_att = d_att.astype(jnp.bfloat16)
    do_ref[...] = d_att
    d_att = d_att.astype(jnp.float32)
    delta = jnp.sum(d_att * attended, axis=0, keepdims=True)
    delta_ref[...] = jnp.broadcast_to(delta, (8, ROWS))
    root_ref[...] = jnp.broadcast_to(inv_root, (8, BLK))
    do_t, delta = scaled_upstream(d_att, delta, inv_ref[1:2])
    do_rows = rows_of(do_t)
    q_rows = stacked(q_ref[...])
    copies = []
    for peer in range(PEERS):
        weights = w_ref[peer]
        d_score = score_grad(kv_ref[peer, 1], weights, do_t, delta)
        copies.append(send_terms(peer, weights, d_score, do_rows, q_rows, terms_ref, held, sent))
    for copy in copies:
        copy.wait()


def near_back_kernel(
    q_ref, near_ref, far_ref, w_near_ref, w_far_ref, inv_ref, do_ref, delta_ref, att_ref, root_ref, gain_ref,
    terms_ref, grad_ref, out_ref, held, sent,
):
    d_att = do_ref[...].astype(jnp.float32)
    do_t, delta = scaled_upstream(d_att, delta_ref[0:1], inv_ref[0:1])
    do_rows = rows_of(do_t)
    q_rows = stacked(q_ref[...])
    grad = jnp.zeros((DH, ROWS), jnp.float32)
    copies = []
    for peer in range(PEERS):
        weights = w_near_ref[peer]
        d_score = score_grad(near_ref[peer, 1], weights, do_t, delta)
        copies.append(send_terms(peer, weights, d_score, do_rows, q_rows, terms_ref, held, sent))
        grad = grad + jnp.dot(near_ref[peer, 0].T, d_score, preferred_element_type=jnp.float32)
    do_t, delta = scaled_upstream(d_att, delta_ref[0:1], inv_ref[1:2])
    for peer in range(PEERS):
        d_score = score_grad(far_ref[peer, 1], w_far_ref[peer], do_t, delta)
        grad = grad + jnp.dot(far_ref[peer, 0].T, d_score, preferred_element_type=jnp.float32)
    grad_ref[...] = (unstacked_t(grad) * SCALING).astype(jnp.bfloat16)
    normed = att_ref[...] * to_groups(root_ref[0:1])
    out_ref[...] = (unstacked_t(normed) * gain_ref[...]).astype(jnp.bfloat16)
    for copy in copies:
        copy.wait()


def sums_kernel(place, far_ref, below_ref, above_ref):
    zp, y = place[0], place[1]
    below = jnp.zeros((2, BLK, DH), jnp.float32)
    above = jnp.zeros((2, BLK, DH), jnp.float32)
    for peer in range(PEERS):
        take = jnp.where(zp == peer // 4, y >= peer % 4, zp == 1)
        share = jnp.where(take, 1.0, 0.0)
        term = far_ref[peer].astype(jnp.float32)
        below = below + term * share
        above = above + term * (1.0 - share)
    below_ref[...] = below.astype(jnp.bfloat16)
    above_ref[...] = above.astype(jnp.bfloat16)


def last_kernel(near_ref, below_ref, above_ref, keys_ref, values_ref):
    total = below_ref[...].astype(jnp.float32) + above_ref[...].astype(jnp.float32)
    for peer in range(PEERS):
        total = total + near_ref[peer].astype(jnp.float32)
    keys_ref[...] = total[0].astype(jnp.bfloat16)
    values_ref[...] = total[1].astype(jnp.bfloat16)


def shape(dims, dtype):
    return jax.ShapeDtypeStruct(dims, dtype)


def in_vmem(count):
    return [pl.BlockSpec(memory_space=pltpu.VMEM)] * count


def in_smem(count):
    return [pl.BlockSpec(memory_space=pltpu.SMEM)] * count


def two_planes(array, by):
    length = lax.axis_size("zq")
    return lax.ppermute(array, "zq", [(i, (i + by) % length) for i in range(length)])


def call(kernel, name, outs, smem, vmem, scratch=(), flops=0, size=0, hbm=0):
    specs = tuple([pl.BlockSpec(memory_space=pltpu.HBM)] * hbm + in_vmem(len(outs) - hbm))
    return pl.pallas_call(
        kernel,
        out_shape=tuple(pltpu.HBM(o.shape, o.dtype) for o in outs[:hbm]) + tuple(outs[hbm:]),
        in_specs=in_smem(smem) + in_vmem(vmem),
        out_specs=specs,
        scratch_shapes=list(scratch),
        compiler_params=pltpu.CompilerParams(vmem_limit_bytes=VMEM_LIMIT),
        cost_estimate=pl.CostEstimate(flops=flops, bytes_accessed=size, transcendentals=0),
        name=name,
    )


def per_device(queries, keys_in, values_in, norm_gain, grad_out, nearby_block_mask):
    zp, y = lax.axis_index("zp"), lax.axis_index("y")
    place = jnp.stack([zp, y]).astype(jnp.int32)
    gain = norm_gain.reshape(1, -1)
    bf16, f32 = jnp.bfloat16, jnp.float32
    block = (2, BLK, DH)
    blocks = shape((PEERS, 2, BLK, DH), bf16)
    squares = shape((PEERS, BLK, ROWS), bf16)
    columns = shape((DH, ROWS), f32)
    row = shape((8, ROWS), f32)

    first = jnp.arange(2, dtype=jnp.int32)[:, None, None] == 0
    own = jnp.where(first, keys_in[None], values_in[None])
    above = two_planes(own, -1)
    below = two_planes(own, 1)
    near = lax.all_to_all(jnp.broadcast_to(own[None], (PEERS,) + block), PAIR, 0, 0)
    to_zp = jnp.arange(PEERS, dtype=jnp.int32)[:, None, None, None] // 4
    to_y = jnp.arange(PEERS, dtype=jnp.int32)[:, None, None, None] % 4
    take_below = jnp.where(to_zp == zp, y >= to_y, zp == 1)
    far = lax.all_to_all(jnp.where(take_below, below[None], above[None]), PAIR, 0, 0)

    sending = [pltpu.VMEM((PEERS,) + block, bf16), pltpu.SemaphoreType.DMA((PEERS,))]
    scores = [pltpu.VMEM((PEERS, BLK, ROWS), f32)]
    w_near, numer, upstream, stats = call(
        near_kernel, "near", (squares, columns, columns, row), 2, 4, scores, 280_000_000, 3_000_000
    )(place, nearby_block_mask, queries, near, grad_out, gain)
    w_far, attended, inverse, part = call(
        far_kernel, "far", (squares, columns, row, shape((2, BLK), f32)), 2, 5, scores, 280_000_000, 3_000_000
    )(place, nearby_block_mask, queries, far, numer, upstream, stats)
    sums = lax.all_to_all(jnp.broadcast_to(part[None], (KV_HEADS, 2, BLK)), "head", 0, 0)
    far_terms, d_att, delta, inv_root = call(
        far_back_kernel,
        "far_back",
        (blocks, shape((DH, ROWS), bf16), row, shape((8, BLK), f32)),
        0, 7, sending, 400_000_000, 4_000_000, 1,
    )(queries, far, w_far, attended, upstream, inverse, sums)
    far_back = lax.all_to_all(far_terms, PAIR, 0, 0)
    tall = shape((BLK, GROUP * DH), bf16)
    near_terms, grad_queries, normed_out = call(
        near_back_kernel, "near_back", (blocks, tall, tall), 0, 11, sending, 800_000_000, 6_000_000, 1
    )(queries, near, far, w_near, w_far, inverse, d_att, delta, attended, inv_root, gain)
    near_back = lax.all_to_all(near_terms, PAIR, 0, 0)
    half = shape(block, bf16)
    to_below, to_above = call(sums_kernel, "sums", (half, half), 1, 1, (), 1_000_000, 600_000)(place, far_back)
    from_above = two_planes(to_below, -1)
    from_below = two_planes(to_above, 1)
    piece = shape((BLK, DH), bf16)
    grad_keys, grad_values = call(last_kernel, "last", (piece, piece), 0, 3, (), 1_000_000, 700_000)(
        near_back, from_below, from_above
    )
    return normed_out, grad_queries, grad_keys, grad_values


def solution(mesh):
    spans, heads = mesh.devices.shape
    fine = Mesh(mesh.devices.reshape(spans // 8, 2, 4, heads), ("zq", "zp", "y", "head"))
    seq = ("zq", "zp", "y")
    both = P(seq, "head")
    return jax.shard_map(
        per_device,
        mesh=fine,
        in_specs=(both, both, both, P("head"), both, P(seq, None)),
        out_specs=(both, both, both, both),
        check_vma=False,
    )
```

```python
import math

import jax
import jax.numpy as jnp
from jax import lax
from jax.experimental import pallas as pl
from jax.experimental.pallas import tpu as pltpu
from jax.sharding import Mesh
from jax.sharding import PartitionSpec as P

HEADS = 32
KV_HEADS = 8
GROUP = HEADS // KV_HEADS
DH = 128
BLK = 128
ROWS = GROUP * BLK
PEERS = 8
NEGATIVE = -1e30
EPSILON = 1e-06
FEATURES = HEADS * DH
SCALING = DH ** (-0.5)
EXP2_SCALE = SCALING / math.log(2.0)
PAIR = ("zp", "y")
VMEM_LIMIT = 12 * 1024 * 1024


def window_slot(zp, y, peer, part):
    peer_zp, peer_y = peer // 4, peer % 4
    across = (zp - peer_zp) & 1
    shift = peer_y - y
    if part == 0:
        return 8 + shift + across * (4 * (1 - 2 * zp))
    same = shift & 15
    other = 8 + shift - 4 * (1 - 2 * zp)
    return jnp.where(across == 1, other, same)


def stacked(array):
    return jnp.concatenate([array[:, g * DH : (g + 1) * DH] for g in range(GROUP)], axis=0)


def stacked_t(array):
    return jnp.concatenate([array[:, g * DH : (g + 1) * DH].T for g in range(GROUP)], axis=1)


def unstacked_t(array):
    return jnp.concatenate([array[:, g * BLK : (g + 1) * BLK].T for g in range(GROUP)], axis=1)


def over_groups(row):
    return sum(row[:, g * BLK : (g + 1) * BLK] for g in range(GROUP))


def to_groups(row):
    return jnp.concatenate([row] * GROUP, axis=1)


def forward_kernel(mask, q_ref, kv_ref, up_ref, gain_ref, w_ref, att_ref, up_out, inv_ref, part_ref, s_ref):
    zp, y = lax.axis_index("zp"), lax.axis_index("y")
    q_t = stacked_t(q_ref[...])
    top = jnp.full((8, ROWS), NEGATIVE, jnp.float32)
    for slot in range(2 * PEERS):
        peer, part = slot // 2, slot % 2
        bias = jnp.where(mask[0, window_slot(zp, y, peer, part)] > 0, 0.0, NEGATIVE)
        raw = jnp.dot(kv_ref[peer, part, 0], q_t, preferred_element_type=jnp.float32) + bias
        s_ref[slot] = raw
        top = jnp.maximum(top, raw.reshape(BLK // 8, 8, ROWS).max(axis=0))
    top = top.max(axis=0, keepdims=True)
    total = jnp.zeros((8, ROWS), jnp.float32)
    numer = jnp.zeros((DH, ROWS), jnp.float32)
    for slot in range(2 * PEERS):
        weights = jnp.exp2((s_ref[slot] - top) * EXP2_SCALE)
        total = total + weights.reshape(BLK // 8, 8, ROWS).sum(axis=0)
        rounded = weights.astype(jnp.bfloat16)
        w_ref[slot // 2, slot % 2] = rounded
        values_t = kv_ref[slot // 2, slot % 2, 1].T
        numer = numer + jnp.dot(values_t, rounded, preferred_element_type=jnp.float32)
    inverse = 1.0 / total.sum(axis=0, keepdims=True)
    attended = numer * inverse
    att_ref[...] = attended
    inv_ref[...] = jnp.broadcast_to(inverse, (8, ROWS))
    upstream = stacked_t(up_ref[...].astype(jnp.float32) * gain_ref[...])
    up_out[...] = upstream
    squares = over_groups(jnp.sum(attended * attended, axis=0, keepdims=True))
    products = over_groups(jnp.sum(upstream * attended, axis=0, keepdims=True))
    part_ref[...] = jnp.concatenate([squares, products], axis=0)


def rows_of(do_t):
    return jnp.concatenate([do_t[:, g * BLK : (g + 1) * BLK].T for g in range(GROUP)], axis=0)


def backward_kernel(q_ref, kv_ref, w_ref, att_ref, up_ref, inv_ref, sums_ref, terms_ref, grad_ref, normed_ref):
    sums = sums_ref[0]
    for peer in range(1, KV_HEADS):
        sums = sums + sums_ref[peer]
    root = jnp.sqrt(sums[0:1] / FEATURES + EPSILON)
    inv_root = 1.0 / root
    inner = sums[1:2] * inv_root
    attended = att_ref[...]
    normed = attended * to_groups(inv_root)
    normed_ref[...] = normed
    d_att = (up_ref[...] - normed * to_groups(inner / FEATURES)) * to_groups(inv_root)
    d_att = d_att.astype(jnp.bfloat16).astype(jnp.float32)
    inverse = inv_ref[0:1]
    delta = jnp.sum(d_att * attended, axis=0, keepdims=True) * inverse
    do_t = (d_att * inverse).astype(jnp.bfloat16)
    do_rows = rows_of(do_t)
    q_rows = stacked(q_ref[...])
    grad = jnp.zeros((DH, ROWS), jnp.float32)
    for slot in range(2 * PEERS):
        peer, part = slot // 2, slot % 2
        weights = w_ref[peer, part]
        d_prob = jnp.dot(kv_ref[peer, part, 1], do_t, preferred_element_type=jnp.float32)
        d_score = (weights.astype(jnp.float32) * (d_prob - delta)).astype(jnp.bfloat16)
        term_k = jnp.dot(d_score, q_rows, preferred_element_type=jnp.float32) * SCALING
        term_v = jnp.dot(weights, do_rows, preferred_element_type=jnp.float32)
        terms_ref[peer, part, 0] = term_k.astype(jnp.bfloat16)
        terms_ref[peer, part, 1] = term_v.astype(jnp.bfloat16)
        grad = grad + jnp.dot(kv_ref[peer, part, 0].T, d_score, preferred_element_type=jnp.float32)
    grad_ref[...] = grad


def far_sums_kernel(terms_ref, below_ref, above_ref):
    zp, y = lax.axis_index("zp"), lax.axis_index("y")
    below = jnp.zeros((2, BLK, DH), jnp.float32)
    above = jnp.zeros((2, BLK, DH), jnp.float32)
    for peer in range(PEERS):
        take = jnp.where(zp == peer // 4, y >= peer % 4, zp == 1)
        share = jnp.where(take, 1.0, 0.0)
        term = terms_ref[peer, 1].astype(jnp.float32)
        below = below + term * share
        above = above + term * (1.0 - share)
    below_ref[...] = below.astype(jnp.bfloat16)
    above_ref[...] = above.astype(jnp.bfloat16)


def near_sums_kernel(terms_ref, grad_ref, normed_ref, gain_ref, sum_ref, grad_out, out_ref):
    total = jnp.zeros((2, BLK, DH), jnp.float32)
    for peer in range(PEERS):
        total = total + terms_ref[peer, 0].astype(jnp.float32)
    sum_ref[...] = total
    grad_out[...] = (unstacked_t(grad_ref[...]) * SCALING).astype(jnp.bfloat16)
    out_ref[...] = (unstacked_t(normed_ref[...]) * gain_ref[...]).astype(jnp.bfloat16)


def last_kernel(near_ref, below_ref, above_ref, keys_ref, values_ref):
    total = near_ref[...] + below_ref[...].astype(jnp.float32) + above_ref[...].astype(jnp.float32)
    keys_ref[...] = total[0].astype(jnp.bfloat16)
    values_ref[...] = total[1].astype(jnp.bfloat16)


def shape(dims, dtype):
    return jax.ShapeDtypeStruct(dims, dtype)


def in_vmem(count):
    return [pl.BlockSpec(memory_space=pltpu.VMEM)] * count


def in_smem(count):
    return [pl.BlockSpec(memory_space=pltpu.SMEM)] * count


def two_planes(array, by):
    length = lax.axis_size("zq")
    return lax.ppermute(array, "zq", [(i, (i + by) % length) for i in range(length)])


def call(kernel, name, outs, smem, vmem, scratch=(), flops=0, size=0):
    specs = tuple(in_vmem(len(outs)))
    return pl.pallas_call(
        kernel,
        out_shape=tuple(outs),
        in_specs=in_smem(smem) + in_vmem(vmem),
        out_specs=specs,
        scratch_shapes=list(scratch),
        compiler_params=pltpu.CompilerParams(vmem_limit_bytes=VMEM_LIMIT),
        cost_estimate=pl.CostEstimate(flops=flops, bytes_accessed=size, transcendentals=0),
        name=name,
    )


def per_device(queries, keys_in, values_in, norm_gain, grad_out, nearby_block_mask):
    zp, y = lax.axis_index("zp"), lax.axis_index("y")
    gain = norm_gain.reshape(1, -1)
    bf16, f32 = jnp.bfloat16, jnp.float32
    block = (2, BLK, DH)
    columns = shape((DH, ROWS), f32)
    row = shape((8, ROWS), f32)

    first = jnp.arange(2, dtype=jnp.int32)[:, None, None] == 0
    own = jnp.where(first, keys_in[None], values_in[None])
    above = two_planes(own, -1)
    below = two_planes(own, 1)
    index = jnp.arange(2 * PEERS, dtype=jnp.int32).reshape(PEERS, 2, 1, 1, 1)
    to_zp, to_y = index // 8, index // 2 % 4
    take_below = jnp.where(to_zp == zp, y >= to_y, zp == 1)
    chosen = jnp.where(take_below, below[None, None], above[None, None])
    gathered = lax.all_to_all(jnp.where(index % 2 == 0, own[None, None], chosen), PAIR, 0, 0)

    scores = [pltpu.VMEM((2 * PEERS, BLK, ROWS), f32)]
    weights, attended, upstream, inverse, part = call(
        forward_kernel,
        "forward",
        (shape((PEERS, 2, BLK, ROWS), bf16), columns, columns, row, shape((2, BLK), f32)),
        1, 4, scores, 550_000_000, 5_000_000,
    )(nearby_block_mask, queries, gathered, grad_out, gain)
    sums = lax.all_to_all(jnp.broadcast_to(part[None], (KV_HEADS, 2, BLK)), "head", 0, 0)
    terms, grad_t, normed_t = call(
        backward_kernel,
        "backward",
        (shape((PEERS, 2) + block, bf16), columns, columns),
        0, 7, (), 1_100_000_000, 5_000_000,
    )(queries, gathered, weights, attended, upstream, inverse, sums)
    returned = lax.all_to_all(terms, PAIR, 0, 0)
    half = shape(block, bf16)
    to_below, to_above = call(far_sums_kernel, "far_sums", (half, half), 0, 1, (), 1_000_000, 600_000)(returned)
    from_above = two_planes(to_below, -1)
    from_below = two_planes(to_above, 1)
    tall = shape((BLK, GROUP * DH), bf16)
    near_sum, grad_queries, normed_out = call(
        near_sums_kernel, "near_sums", (shape(block, f32), tall, tall), 0, 4, (), 1_000_000, 1_500_000
    )(returned, grad_t, normed_t, gain)
    piece = shape((BLK, DH), bf16)
    grad_keys, grad_values = call(last_kernel, "last", (piece, piece), 0, 3, (), 1_000_000, 300_000)(
        near_sum, from_below, from_above
    )
    return normed_out, grad_queries, grad_keys, grad_values


def solution(mesh):
    spans, heads = mesh.devices.shape
    fine = Mesh(mesh.devices.reshape(spans // 8, 2, 4, heads), ("zq", "zp", "y", "head"))
    seq = ("zq", "zp", "y")
    both = P(seq, "head")
    return jax.shard_map(
        per_device,
        mesh=fine,
        in_specs=(both, both, both, P("head"), both, P(seq, None)),
        out_specs=(both, both, both, both),
        check_vma=False,
    )
```

```python
import math

import jax
import jax.numpy as jnp
from jax import lax
from jax.experimental import pallas as pl
from jax.experimental.pallas import tpu as pltpu
from jax.sharding import Mesh
from jax.sharding import PartitionSpec as P

HEADS = 32
KV_HEADS = 8
GROUP = HEADS // KV_HEADS
DH = 128
BLK = 128
ROWS = GROUP * BLK
PEERS = 8
FORWARD_STEP = 2
BACKWARD_STEP = 4
NEGATIVE = -1e30
EPSILON = 1e-06
FEATURES = HEADS * DH
SCALING = DH ** (-0.5)
EXP2_SCALE = SCALING / math.log(2.0)
PAIR = ("zp", "y")
VMEM_LIMIT = 12 * 1024 * 1024


def window_slot(zp, y, peer, part):
    peer_zp, peer_y = peer // 4, peer % 4
    across = (zp - peer_zp) & 1
    shift = peer_y - y
    if part == 0:
        return 8 + shift + across * (4 * (1 - 2 * zp))
    same = shift & 15
    other = 8 + shift - 4 * (1 - 2 * zp)
    return jnp.where(across == 1, other, same)


def stacked(array):
    return jnp.concatenate([array[:, g * DH : (g + 1) * DH] for g in range(GROUP)], axis=0)


def stacked_t(array):
    return jnp.concatenate([array[:, g * DH : (g + 1) * DH].T for g in range(GROUP)], axis=1)


def unstacked_t(array):
    return jnp.concatenate([array[:, g * BLK : (g + 1) * BLK].T for g in range(GROUP)], axis=1)


def over_groups(row):
    return sum(row[:, g * BLK : (g + 1) * BLK] for g in range(GROUP))


def to_groups(row):
    return jnp.concatenate([row] * GROUP, axis=1)


def joined(ref, first, count, which):
    return jnp.concatenate([ref[slot // 2, slot % 2, which] for slot in range(first, first + count)], axis=0)


def forward_kernel(mask, q_ref, kv_ref, up_ref, gain_ref, w_ref, att_ref, up_out, inv_ref, part_ref, s_ref):
    zp, y = lax.axis_index("zp"), lax.axis_index("y")
    q_t = stacked_t(q_ref[...])
    top = jnp.full((8, ROWS), NEGATIVE, jnp.float32)
    for first in range(0, 2 * PEERS, FORWARD_STEP):
        raw = jnp.dot(joined(kv_ref, first, FORWARD_STEP, 0), q_t, preferred_element_type=jnp.float32)
        for step in range(FORWARD_STEP):
            slot = first + step
            bias = jnp.where(mask[0, window_slot(zp, y, slot // 2, slot % 2)] > 0, 0.0, NEGATIVE)
            block = raw[step * BLK : (step + 1) * BLK] + bias
            s_ref[slot] = block
            top = jnp.maximum(top, block.reshape(BLK // 8, 8, ROWS).max(axis=0))
    top = top.max(axis=0, keepdims=True)
    total = jnp.zeros((8, ROWS), jnp.float32)
    numer = jnp.zeros((DH, ROWS), jnp.float32)
    for first in range(0, 2 * PEERS, FORWARD_STEP):
        for slot in range(first, first + FORWARD_STEP):
            weights = jnp.exp2((s_ref[slot] - top) * EXP2_SCALE)
            total = total + weights.reshape(BLK // 8, 8, ROWS).sum(axis=0)
            w_ref[slot] = weights.astype(jnp.bfloat16)
        rounded = w_ref[first : first + FORWARD_STEP].reshape(FORWARD_STEP * BLK, ROWS)
        values_t = joined(kv_ref, first, FORWARD_STEP, 1).T
        numer = numer + jnp.dot(values_t, rounded, preferred_element_type=jnp.float32)
    inverse = 1.0 / total.sum(axis=0, keepdims=True)
    attended = numer * inverse
    att_ref[...] = attended
    inv_ref[...] = jnp.broadcast_to(inverse, (8, ROWS))
    upstream = stacked_t(up_ref[...].astype(jnp.float32) * gain_ref[...])
    up_out[...] = upstream
    squares = over_groups(jnp.sum(attended * attended, axis=0, keepdims=True))
    products = over_groups(jnp.sum(upstream * attended, axis=0, keepdims=True))
    part_ref[...] = jnp.concatenate([squares, products], axis=0)


def rows_of(do_t):
    return jnp.concatenate([do_t[:, g * BLK : (g + 1) * BLK].T for g in range(GROUP)], axis=0)


def backward_kernel(q_ref, kv_ref, w_ref, att_ref, up_ref, inv_ref, sums_ref, terms_ref, grad_ref, normed_ref):
    sums = sums_ref[0]
    for peer in range(1, KV_HEADS):
        sums = sums + sums_ref[peer]
    root = jnp.sqrt(sums[0:1] / FEATURES + EPSILON)
    inv_root = 1.0 / root
    inner = sums[1:2] * inv_root
    attended = att_ref[...]
    normed = attended * to_groups(inv_root)
    normed_ref[...] = normed
    d_att = (up_ref[...] - normed * to_groups(inner / FEATURES)) * to_groups(inv_root)
    d_att = d_att.astype(jnp.bfloat16).astype(jnp.float32)
    inverse = inv_ref[0:1]
    delta = jnp.sum(d_att * attended, axis=0, keepdims=True) * inverse
    do_t = (d_att * inverse).astype(jnp.bfloat16)
    do_rows = rows_of(do_t)
    q_rows = stacked(q_ref[...])
    grad = jnp.zeros((DH, ROWS), jnp.float32)
    for first in range(0, 2 * PEERS, BACKWARD_STEP):
        weights = w_ref[first : first + BACKWARD_STEP].reshape(BACKWARD_STEP * BLK, ROWS)
        d_prob = jnp.dot(joined(kv_ref, first, BACKWARD_STEP, 1), do_t, preferred_element_type=jnp.float32)
        d_score = (weights.astype(jnp.float32) * (d_prob - delta)).astype(jnp.bfloat16)
        term_k = (jnp.dot(d_score, q_rows, preferred_element_type=jnp.float32) * SCALING).astype(jnp.bfloat16)
        term_v = jnp.dot(weights, do_rows, preferred_element_type=jnp.float32).astype(jnp.bfloat16)
        for step in range(BACKWARD_STEP):
            slot = first + step
            terms_ref[slot // 2, slot % 2, 0] = term_k[step * BLK : (step + 1) * BLK]
            terms_ref[slot // 2, slot % 2, 1] = term_v[step * BLK : (step + 1) * BLK]
        keys_t = joined(kv_ref, first, BACKWARD_STEP, 0).T
        grad = grad + jnp.dot(keys_t, d_score, preferred_element_type=jnp.float32)
    grad_ref[...] = grad


def far_sums_kernel(terms_ref, first_ref, second_ref):
    zp, y = lax.axis_index("zp"), lax.axis_index("y")
    odd = lax.axis_index("zq") % 2
    first = jnp.zeros((2, BLK, DH), jnp.float32)
    second = jnp.zeros((2, BLK, DH), jnp.float32)
    for peer in range(PEERS):
        below = jnp.where(jnp.where(zp == peer // 4, y >= peer % 4, zp == 1), 1, 0)
        share = jnp.where(below == odd, 1.0, 0.0)
        term = terms_ref[peer, 1].astype(jnp.float32)
        first = first + term * share
        second = second + term * (1.0 - share)
    first_ref[...] = first.astype(jnp.bfloat16)
    second_ref[...] = second.astype(jnp.bfloat16)


def near_sums_kernel(terms_ref, grad_ref, normed_ref, gain_ref, sum_ref, grad_out, out_ref):
    total = jnp.zeros((2, BLK, DH), jnp.float32)
    for peer in range(PEERS):
        total = total + terms_ref[peer, 0].astype(jnp.float32)
    sum_ref[...] = total
    grad_out[...] = (unstacked_t(grad_ref[...]) * SCALING).astype(jnp.bfloat16)
    out_ref[...] = (unstacked_t(normed_ref[...]) * gain_ref[...]).astype(jnp.bfloat16)


def last_kernel(near_ref, first_ref, second_ref, keys_ref, values_ref):
    total = near_ref[...] + first_ref[...].astype(jnp.float32) + second_ref[...].astype(jnp.float32)
    keys_ref[...] = total[0].astype(jnp.bfloat16)
    values_ref[...] = total[1].astype(jnp.bfloat16)


def shape(dims, dtype):
    return jax.ShapeDtypeStruct(dims, dtype)


def in_vmem(count):
    return [pl.BlockSpec(memory_space=pltpu.VMEM)] * count


def in_smem(count):
    return [pl.BlockSpec(memory_space=pltpu.SMEM)] * count


def swapped(array, first):
    length = lax.axis_size("zq")
    pairs = []
    for low in range(0 if first else 1, length - 1, 2):
        pairs += [(low, low + 1), (low + 1, low)]
    return lax.ppermute(array, "zq", pairs)


def call(kernel, name, outs, smem, vmem, scratch=(), flops=0, size=0):
    specs = tuple(in_vmem(len(outs)))
    return pl.pallas_call(
        kernel,
        out_shape=tuple(outs),
        in_specs=in_smem(smem) + in_vmem(vmem),
        out_specs=specs,
        scratch_shapes=list(scratch),
        compiler_params=pltpu.CompilerParams(vmem_limit_bytes=VMEM_LIMIT),
        cost_estimate=pl.CostEstimate(flops=flops, bytes_accessed=size, transcendentals=0),
        name=name,
    )


def per_device(queries, keys_in, values_in, norm_gain, grad_out, nearby_block_mask):
    zp, y = lax.axis_index("zp"), lax.axis_index("y")
    gain = norm_gain.reshape(1, -1)
    bf16, f32 = jnp.bfloat16, jnp.float32
    block = (2, BLK, DH)
    columns = shape((DH, ROWS), f32)
    row = shape((8, ROWS), f32)

    first = jnp.arange(2, dtype=jnp.int32)[:, None, None] == 0
    own = jnp.where(first, keys_in[None], values_in[None])
    got_first = swapped(own, True)
    got_second = swapped(own, False)
    index = jnp.arange(2 * PEERS, dtype=jnp.int32).reshape(PEERS, 2, 1, 1, 1)
    to_zp, to_y = index // 8, index // 2 % 4
    take_below = jnp.where(to_zp == zp, y >= to_y, zp == 1)
    odd = lax.axis_index("zq") % 2 == 1
    chosen = jnp.where(take_below == odd, got_first[None, None], got_second[None, None])
    gathered = lax.all_to_all(jnp.where(index % 2 == 0, own[None, None], chosen), PAIR, 0, 0)

    scores = [pltpu.VMEM((2 * PEERS, BLK, ROWS), f32)]
    weights, attended, upstream, inverse, part = call(
        forward_kernel,
        "forward",
        (shape((2 * PEERS, BLK, ROWS), bf16), columns, columns, row, shape((2, BLK), f32)),
        1, 4, scores, 550_000_000, 5_000_000,
    )(nearby_block_mask, queries, gathered, grad_out, gain)
    sums = lax.all_to_all(jnp.broadcast_to(part[None], (KV_HEADS, 2, BLK)), "head", 0, 0)
    terms, grad_t, normed_t = call(
        backward_kernel,
        "backward",
        (shape((PEERS, 2) + block, bf16), columns, columns),
        0, 7, (), 1_100_000_000, 5_000_000,
    )(queries, gathered, weights, attended, upstream, inverse, sums)
    returned = lax.all_to_all(terms, PAIR, 0, 0)
    half = shape(block, bf16)
    to_first, to_second = call(far_sums_kernel, "far_sums", (half, half), 0, 1, (), 1_000_000, 600_000)(returned)
    from_first = swapped(to_first, True)
    from_second = swapped(to_second, False)
    tall = shape((BLK, GROUP * DH), bf16)
    near_sum, grad_queries, normed_out = call(
        near_sums_kernel, "near_sums", (shape(block, f32), tall, tall), 0, 4, (), 1_000_000, 1_500_000
    )(returned, grad_t, normed_t, gain)
    piece = shape((BLK, DH), bf16)
    grad_keys, grad_values = call(last_kernel, "last", (piece, piece), 0, 3, (), 1_000_000, 300_000)(
        near_sum, from_first, from_second
    )
    return normed_out, grad_queries, grad_keys, grad_values


def solution(mesh):
    spans, heads = mesh.devices.shape
    fine = Mesh(mesh.devices.reshape(spans // 8, 2, 4, heads), ("zq", "zp", "y", "head"))
    seq = ("zq", "zp", "y")
    both = P(seq, "head")
    return jax.shard_map(
        per_device,
        mesh=fine,
        in_specs=(both, both, both, P("head"), both, P(seq, None)),
        out_specs=(both, both, both, both),
        check_vma=False,
    )
```

```python
import math

import jax
import jax.numpy as jnp
from jax import lax
from jax.experimental import pallas as pl
from jax.experimental.pallas import tpu as pltpu
from jax.sharding import Mesh
from jax.sharding import PartitionSpec as P

HEADS = 32
KV_HEADS = 8
GROUP = HEADS // KV_HEADS
DH = 128
BLK = 128
ROWS = GROUP * BLK
PEERS = 8
FORWARD_STEP = 2
BACKWARD_STEP = 4
NEGATIVE = -1e30
EPSILON = 1e-06
FEATURES = HEADS * DH
SCALING = DH ** (-0.5)
EXP2_SCALE = SCALING / math.log(2.0)
PAIR = ("zp", "y")
VMEM_LIMIT = 12 * 1024 * 1024


def window_slot(zp, y, peer, part):
    peer_zp, peer_y = peer // 4, peer % 4
    across = (zp - peer_zp) & 1
    shift = peer_y - y
    if part == 0:
        return 8 + shift + across * (4 * (1 - 2 * zp))
    same = shift & 15
    other = 8 + shift - 4 * (1 - 2 * zp)
    return jnp.where(across == 1, other, same)


def stacked(array):
    return jnp.concatenate([array[:, g * DH : (g + 1) * DH] for g in range(GROUP)], axis=0)


def stacked_t(array):
    return jnp.concatenate([array[:, g * DH : (g + 1) * DH].T for g in range(GROUP)], axis=1)


def unstacked_t(array):
    return jnp.concatenate([array[:, g * BLK : (g + 1) * BLK].T for g in range(GROUP)], axis=1)


def over_groups(row):
    return sum(row[:, g * BLK : (g + 1) * BLK] for g in range(GROUP))


def to_groups(row):
    return jnp.concatenate([row] * GROUP, axis=1)


def joined(ref, first, count, which):
    return jnp.concatenate([ref[slot // 2, slot % 2, which] for slot in range(first, first + count)], axis=0)


def forward_kernel(mask, q_ref, kv_ref, up_ref, gain_ref, w_ref, att_ref, up_out, inv_ref, part_ref, s_ref):
    zp, y = lax.axis_index("zp"), lax.axis_index("y")
    q_t = stacked_t(q_ref[...])
    top = jnp.full((8, ROWS), NEGATIVE, jnp.float32)
    for first in range(0, 2 * PEERS, FORWARD_STEP):
        raw = jnp.dot(joined(kv_ref, first, FORWARD_STEP, 0), q_t, preferred_element_type=jnp.float32)
        for step in range(FORWARD_STEP):
            slot = first + step
            bias = jnp.where(mask[0, window_slot(zp, y, slot // 2, slot % 2)] > 0, 0.0, NEGATIVE)
            block = raw[step * BLK : (step + 1) * BLK] + bias
            s_ref[slot] = block
            top = jnp.maximum(top, block.reshape(BLK // 8, 8, ROWS).max(axis=0))
    top = top.max(axis=0, keepdims=True)
    total = jnp.zeros((8, ROWS), jnp.float32)
    numer = jnp.zeros((DH, ROWS), jnp.float32)
    for first in range(0, 2 * PEERS, FORWARD_STEP):
        for slot in range(first, first + FORWARD_STEP):
            weights = jnp.exp2((s_ref[slot] - top) * EXP2_SCALE)
            total = total + weights.reshape(BLK // 8, 8, ROWS).sum(axis=0)
            w_ref[slot] = weights.astype(jnp.bfloat16)
        rounded = w_ref[first : first + FORWARD_STEP].reshape(FORWARD_STEP * BLK, ROWS)
        values_t = joined(kv_ref, first, FORWARD_STEP, 1).T
        numer = numer + jnp.dot(values_t, rounded, preferred_element_type=jnp.float32)
    inverse = 1.0 / total.sum(axis=0, keepdims=True)
    attended = numer * inverse
    att_ref[...] = attended
    inv_ref[...] = jnp.broadcast_to(inverse, (8, ROWS))
    upstream = stacked_t(up_ref[...].astype(jnp.float32) * gain_ref[...])
    up_out[...] = upstream
    squares = over_groups(jnp.sum(attended * attended, axis=0, keepdims=True))
    products = over_groups(jnp.sum(upstream * attended, axis=0, keepdims=True))
    part_ref[...] = jnp.concatenate([squares, products], axis=0)


def rows_of(do_t):
    return jnp.concatenate([do_t[:, g * BLK : (g + 1) * BLK].T for g in range(GROUP)], axis=0)


def backward_kernel(q_ref, kv_ref, w_ref, att_ref, up_ref, inv_ref, sums_ref, terms_ref, grad_ref, normed_ref):
    sums = sums_ref[0]
    for peer in range(1, KV_HEADS):
        sums = sums + sums_ref[peer]
    root = jnp.sqrt(sums[0:1] / FEATURES + EPSILON)
    inv_root = 1.0 / root
    inner = sums[1:2] * inv_root
    attended = att_ref[...]
    normed = attended * to_groups(inv_root)
    normed_ref[...] = normed
    d_att = (up_ref[...] - normed * to_groups(inner / FEATURES)) * to_groups(inv_root)
    d_att = d_att.astype(jnp.bfloat16).astype(jnp.float32)
    inverse = inv_ref[0:1]
    delta = jnp.sum(d_att * attended, axis=0, keepdims=True) * inverse
    do_t = (d_att * inverse).astype(jnp.bfloat16)
    do_rows = rows_of(do_t)
    q_rows = stacked(q_ref[...])
    grad = jnp.zeros((DH, ROWS), jnp.float32)
    for first in range(0, 2 * PEERS, BACKWARD_STEP):
        weights = w_ref[first : first + BACKWARD_STEP].reshape(BACKWARD_STEP * BLK, ROWS)
        d_prob = jnp.dot(joined(kv_ref, first, BACKWARD_STEP, 1), do_t, preferred_element_type=jnp.float32)
        d_score = (weights.astype(jnp.float32) * (d_prob - delta)).astype(jnp.bfloat16)
        term_k = (jnp.dot(d_score, q_rows, preferred_element_type=jnp.float32) * SCALING).astype(jnp.bfloat16)
        term_v = jnp.dot(weights, do_rows, preferred_element_type=jnp.float32).astype(jnp.bfloat16)
        for step in range(BACKWARD_STEP):
            slot = first + step
            terms_ref[slot // 2, slot % 2, 0] = term_k[step * BLK : (step + 1) * BLK]
            terms_ref[slot // 2, slot % 2, 1] = term_v[step * BLK : (step + 1) * BLK]
        keys_t = joined(kv_ref, first, BACKWARD_STEP, 0).T
        grad = grad + jnp.dot(keys_t, d_score, preferred_element_type=jnp.float32)
    grad_ref[...] = grad


def far_sums_kernel(terms_ref, first_ref, second_ref):
    zp, y = lax.axis_index("zp"), lax.axis_index("y")
    odd = lax.axis_index("zq") % 2
    first = jnp.zeros((2, BLK, DH), jnp.float32)
    second = jnp.zeros((2, BLK, DH), jnp.float32)
    for peer in range(PEERS):
        below = jnp.where(jnp.where(zp == peer // 4, y >= peer % 4, zp == 1), 1, 0)
        share = jnp.where(below == odd, 1.0, 0.0)
        term = terms_ref[peer, 1].astype(jnp.float32)
        first = first + term * share
        second = second + term * (1.0 - share)
    first_ref[...] = first.astype(jnp.bfloat16)
    second_ref[...] = second.astype(jnp.bfloat16)


def near_sums_kernel(terms_ref, grad_ref, normed_ref, gain_ref, sum_ref, grad_out, out_ref):
    total = jnp.zeros((2, BLK, DH), jnp.float32)
    for peer in range(PEERS):
        total = total + terms_ref[peer, 0].astype(jnp.float32)
    sum_ref[...] = total
    grad_out[...] = (unstacked_t(grad_ref[...]) * SCALING).astype(jnp.bfloat16)
    out_ref[...] = (unstacked_t(normed_ref[...]) * gain_ref[...]).astype(jnp.bfloat16)


def last_kernel(near_ref, first_ref, second_ref, keys_ref, values_ref):
    total = near_ref[...] + first_ref[...].astype(jnp.float32) + second_ref[...].astype(jnp.float32)
    keys_ref[...] = total[0].astype(jnp.bfloat16)
    values_ref[...] = total[1].astype(jnp.bfloat16)


def shape(dims, dtype):
    return jax.ShapeDtypeStruct(dims, dtype)


def in_vmem(count):
    return [pl.BlockSpec(memory_space=pltpu.VMEM)] * count


def in_smem(count):
    return [pl.BlockSpec(memory_space=pltpu.SMEM)] * count


def swapped(array, first):
    length = lax.axis_size("zq")
    pairs = []
    for low in range(0 if first else 1, length - 1, 2):
        pairs += [(low, low + 1), (low + 1, low)]
    return lax.ppermute(array, "zq", pairs)


def two_planes(array, by):
    length = lax.axis_size("zq")
    return lax.ppermute(array, "zq", [(i, i + by) for i in range(length) if 0 <= i + by < length])


def call(kernel, name, outs, smem, vmem, scratch=(), flops=0, size=0):
    specs = tuple(in_vmem(len(outs)))
    return pl.pallas_call(
        kernel,
        out_shape=tuple(outs),
        in_specs=in_smem(smem) + in_vmem(vmem),
        out_specs=specs,
        scratch_shapes=list(scratch),
        compiler_params=pltpu.CompilerParams(vmem_limit_bytes=VMEM_LIMIT),
        cost_estimate=pl.CostEstimate(flops=flops, bytes_accessed=size, transcendentals=0),
        name=name,
    )


def per_device(queries, keys_in, values_in, norm_gain, grad_out, nearby_block_mask):
    zp, y = lax.axis_index("zp"), lax.axis_index("y")
    gain = norm_gain.reshape(1, -1)
    bf16, f32 = jnp.bfloat16, jnp.float32
    block = (2, BLK, DH)
    columns = shape((DH, ROWS), f32)
    row = shape((8, ROWS), f32)

    first = jnp.arange(2, dtype=jnp.int32)[:, None, None] == 0
    own = jnp.where(first, keys_in[None], values_in[None])
    above = two_planes(own, -1)
    below = two_planes(own, 1)
    index = jnp.arange(2 * PEERS, dtype=jnp.int32).reshape(PEERS, 2, 1, 1, 1)
    to_zp, to_y = index // 8, index // 2 % 4
    take_below = jnp.where(to_zp == zp, y >= to_y, zp == 1)
    chosen = jnp.where(take_below, below[None, None], above[None, None])
    gathered = lax.all_to_all(jnp.where(index % 2 == 0, own[None, None], chosen), PAIR, 0, 0)

    scores = [pltpu.VMEM((2 * PEERS, BLK, ROWS), f32)]
    weights, attended, upstream, inverse, part = call(
        forward_kernel,
        "forward",
        (shape((2 * PEERS, BLK, ROWS), bf16), columns, columns, row, shape((2, BLK), f32)),
        1, 4, scores, 550_000_000, 5_000_000,
    )(nearby_block_mask, queries, gathered, grad_out, gain)
    sums = lax.all_to_all(jnp.broadcast_to(part[None], (KV_HEADS, 2, BLK)), "head", 0, 0)
    terms, grad_t, normed_t = call(
        backward_kernel,
        "backward",
        (shape((PEERS, 2) + block, bf16), columns, columns),
        0, 7, (), 1_100_000_000, 5_000_000,
    )(queries, gathered, weights, attended, upstream, inverse, sums)
    returned = lax.all_to_all(terms, PAIR, 0, 0)
    half = shape(block, bf16)
    to_first, to_second = call(far_sums_kernel, "far_sums", (half, half), 0, 1, (), 1_000_000, 600_000)(returned)
    from_first = swapped(to_first, True)
    from_second = swapped(to_second, False)
    tall = shape((BLK, GROUP * DH), bf16)
    near_sum, grad_queries, normed_out = call(
        near_sums_kernel, "near_sums", (shape(block, f32), tall, tall), 0, 4, (), 1_000_000, 1_500_000
    )(returned, grad_t, normed_t, gain)
    piece = shape((BLK, DH), bf16)
    grad_keys, grad_values = call(last_kernel, "last", (piece, piece), 0, 3, (), 1_000_000, 300_000)(
        near_sum, from_first, from_second
    )
    return normed_out, grad_queries, grad_keys, grad_values


def solution(mesh):
    spans, heads = mesh.devices.shape
    fine = Mesh(mesh.devices.reshape(spans // 8, 2, 4, heads), ("zq", "zp", "y", "head"))
    seq = ("zq", "zp", "y")
    both = P(seq, "head")
    return jax.shard_map(
        per_device,
        mesh=fine,
        in_specs=(both, both, both, P("head"), both, P(seq, None)),
        out_specs=(both, both, both, both),
        check_vma=False,
    )
```

```python
import math

import jax
import jax.numpy as jnp
from jax import lax
from jax.experimental import pallas as pl
from jax.experimental.pallas import tpu as pltpu
from jax.sharding import Mesh
from jax.sharding import PartitionSpec as P

HEADS = 32
KV_HEADS = 8
GROUP = HEADS // KV_HEADS
DH = 128
BLK = 128
ROWS = GROUP * BLK
PEERS = 8
FORWARD_STEP = 2
BACKWARD_STEP = 4
NEGATIVE = -1e30
EPSILON = 1e-06
FEATURES = HEADS * DH
SCALING = DH ** (-0.5)
EXP2_SCALE = SCALING / math.log(2.0)
PAIR = ("zp", "y")
VMEM_LIMIT = 12 * 1024 * 1024


def window_slot(zp, y, peer, part):
    peer_zp, peer_y = peer // 4, peer % 4
    across = (zp - peer_zp) & 1
    shift = peer_y - y
    if part == 0:
        return 8 + shift + across * (4 * (1 - 2 * zp))
    same = shift & 15
    other = 8 + shift - 4 * (1 - 2 * zp)
    return jnp.where(across == 1, other, same)


def stacked(array):
    return jnp.concatenate([array[:, g * DH : (g + 1) * DH] for g in range(GROUP)], axis=0)


def stacked_t(array):
    return jnp.concatenate([array[:, g * DH : (g + 1) * DH].T for g in range(GROUP)], axis=1)


def unstacked_t(array):
    return jnp.concatenate([array[:, g * BLK : (g + 1) * BLK].T for g in range(GROUP)], axis=1)


def over_groups(row):
    return sum(row[:, g * BLK : (g + 1) * BLK] for g in range(GROUP))


def to_groups(row):
    return jnp.concatenate([row] * GROUP, axis=1)


def joined(ref, first, count, which):
    return jnp.concatenate([ref[slot // 2, slot % 2, which] for slot in range(first, first + count)], axis=0)


def forward_kernel(mask, q_ref, kv_ref, up_ref, gain_ref, w_ref, att_ref, up_out, inv_ref, part_ref, s_ref):
    zp, y = lax.axis_index("zp"), lax.axis_index("y")
    q_t = stacked_t(q_ref[...])
    top = jnp.full((8, ROWS), NEGATIVE, jnp.float32)
    for first in range(0, 2 * PEERS, FORWARD_STEP):
        raw = jnp.dot(joined(kv_ref, first, FORWARD_STEP, 0), q_t, preferred_element_type=jnp.float32)
        for step in range(FORWARD_STEP):
            slot = first + step
            bias = jnp.where(mask[0, window_slot(zp, y, slot // 2, slot % 2)] > 0, 0.0, NEGATIVE)
            block = raw[step * BLK : (step + 1) * BLK] + bias
            s_ref[slot] = block
            top = jnp.maximum(top, block.reshape(BLK // 8, 8, ROWS).max(axis=0))
    top = top.max(axis=0, keepdims=True)
    total = jnp.zeros((8, ROWS), jnp.float32)
    numer = jnp.zeros((DH, ROWS), jnp.float32)
    for first in range(0, 2 * PEERS, FORWARD_STEP):
        for slot in range(first, first + FORWARD_STEP):
            weights = jnp.exp2((s_ref[slot] - top) * EXP2_SCALE)
            total = total + weights.reshape(BLK // 8, 8, ROWS).sum(axis=0)
            w_ref[slot] = weights.astype(jnp.bfloat16)
        rounded = w_ref[first : first + FORWARD_STEP].reshape(FORWARD_STEP * BLK, ROWS)
        values_t = joined(kv_ref, first, FORWARD_STEP, 1).T
        numer = numer + jnp.dot(values_t, rounded, preferred_element_type=jnp.float32)
    inverse = 1.0 / total.sum(axis=0, keepdims=True)
    attended = numer * inverse
    att_ref[...] = attended
    inv_ref[...] = jnp.broadcast_to(inverse, (8, ROWS))
    upstream = stacked_t(up_ref[...].astype(jnp.float32) * gain_ref[...])
    up_out[...] = upstream
    squares = over_groups(jnp.sum(attended * attended, axis=0, keepdims=True))
    products = over_groups(jnp.sum(upstream * attended, axis=0, keepdims=True))
    part_ref[...] = jnp.concatenate([squares, products], axis=0)


def rows_of(do_t):
    return jnp.concatenate([do_t[:, g * BLK : (g + 1) * BLK].T for g in range(GROUP)], axis=0)


def backward_kernel(q_ref, kv_ref, w_ref, att_ref, up_ref, inv_ref, sums_ref, terms_ref, grad_ref, normed_ref):
    sums = sums_ref[0]
    for peer in range(1, KV_HEADS):
        sums = sums + sums_ref[peer]
    root = jnp.sqrt(sums[0:1] / FEATURES + EPSILON)
    inv_root = 1.0 / root
    inner = sums[1:2] * inv_root
    attended = att_ref[...]
    normed = attended * to_groups(inv_root)
    normed_ref[...] = normed
    d_att = (up_ref[...] - normed * to_groups(inner / FEATURES)) * to_groups(inv_root)
    d_att = d_att.astype(jnp.bfloat16).astype(jnp.float32)
    inverse = inv_ref[0:1]
    delta = jnp.sum(d_att * attended, axis=0, keepdims=True) * inverse
    do_t = (d_att * inverse).astype(jnp.bfloat16)
    do_rows = rows_of(do_t)
    q_rows = stacked(q_ref[...])
    grad = jnp.zeros((DH, ROWS), jnp.float32)
    for first in range(0, 2 * PEERS, BACKWARD_STEP):
        weights = w_ref[first : first + BACKWARD_STEP].reshape(BACKWARD_STEP * BLK, ROWS)
        d_prob = jnp.dot(joined(kv_ref, first, BACKWARD_STEP, 1), do_t, preferred_element_type=jnp.float32)
        d_score = (weights.astype(jnp.float32) * (d_prob - delta)).astype(jnp.bfloat16)
        term_k = (jnp.dot(d_score, q_rows, preferred_element_type=jnp.float32) * SCALING).astype(jnp.bfloat16)
        term_v = jnp.dot(weights, do_rows, preferred_element_type=jnp.float32).astype(jnp.bfloat16)
        for step in range(BACKWARD_STEP):
            slot = first + step
            terms_ref[slot // 2, slot % 2, 0] = term_k[step * BLK : (step + 1) * BLK]
            terms_ref[slot // 2, slot % 2, 1] = term_v[step * BLK : (step + 1) * BLK]
        keys_t = joined(kv_ref, first, BACKWARD_STEP, 0).T
        grad = grad + jnp.dot(keys_t, d_score, preferred_element_type=jnp.float32)
    grad_ref[...] = grad


def far_sums_kernel(terms_ref, below_ref, above_ref):
    zp, y = lax.axis_index("zp"), lax.axis_index("y")
    below = jnp.zeros((2, BLK, DH), jnp.float32)
    above = jnp.zeros((2, BLK, DH), jnp.float32)
    for peer in range(PEERS):
        take = jnp.where(zp == peer // 4, y >= peer % 4, zp == 1)
        share = jnp.where(take, 1.0, 0.0)
        term = terms_ref[peer, 1].astype(jnp.float32)
        below = below + term * share
        above = above + term * (1.0 - share)
    below_ref[...] = below.astype(jnp.bfloat16)
    above_ref[...] = above.astype(jnp.bfloat16)


def near_sums_kernel(terms_ref, grad_ref, normed_ref, gain_ref, sum_ref, grad_out, out_ref):
    total = jnp.zeros((2, BLK, DH), jnp.float32)
    for peer in range(PEERS):
        total = total + terms_ref[peer, 0].astype(jnp.float32)
    sum_ref[...] = total
    grad_out[...] = (unstacked_t(grad_ref[...]) * SCALING).astype(jnp.bfloat16)
    out_ref[...] = (unstacked_t(normed_ref[...]) * gain_ref[...]).astype(jnp.bfloat16)


def last_kernel(near_ref, above_ref, below_ref, keys_ref, values_ref):
    total = near_ref[...] + below_ref[...].astype(jnp.float32) + above_ref[...].astype(jnp.float32)
    keys_ref[...] = total[0].astype(jnp.bfloat16)
    values_ref[...] = total[1].astype(jnp.bfloat16)


def shape(dims, dtype):
    return jax.ShapeDtypeStruct(dims, dtype)


def in_vmem(count):
    return [pl.BlockSpec(memory_space=pltpu.VMEM)] * count


def in_smem(count):
    return [pl.BlockSpec(memory_space=pltpu.SMEM)] * count


def two_planes(array, by):
    length = lax.axis_size("zq")
    return lax.ppermute(array, "zq", [(i, i + by) for i in range(length) if 0 <= i + by < length])


def call(kernel, name, outs, smem, vmem, scratch=(), flops=0, size=0):
    specs = tuple(in_vmem(len(outs)))
    return pl.pallas_call(
        kernel,
        out_shape=tuple(outs),
        in_specs=in_smem(smem) + in_vmem(vmem),
        out_specs=specs,
        scratch_shapes=list(scratch),
        compiler_params=pltpu.CompilerParams(vmem_limit_bytes=VMEM_LIMIT),
        cost_estimate=pl.CostEstimate(flops=flops, bytes_accessed=size, transcendentals=0),
        name=name,
    )


def per_device(queries, keys_in, values_in, norm_gain, grad_out, nearby_block_mask):
    zp, y = lax.axis_index("zp"), lax.axis_index("y")
    gain = norm_gain.reshape(1, -1)
    bf16, f32 = jnp.bfloat16, jnp.float32
    block = (2, BLK, DH)
    columns = shape((DH, ROWS), f32)
    row = shape((8, ROWS), f32)

    first = jnp.arange(2, dtype=jnp.int32)[:, None, None] == 0
    own = jnp.where(first, keys_in[None], values_in[None])
    above = two_planes(own, -1)
    below = two_planes(own, 1)
    index = jnp.arange(2 * PEERS, dtype=jnp.int32).reshape(PEERS, 2, 1, 1, 1)
    to_zp, to_y = index // 8, index // 2 % 4
    take_below = jnp.where(to_zp == zp, y >= to_y, zp == 1)
    chosen = jnp.where(take_below, below[None, None], above[None, None])
    gathered = lax.all_to_all(jnp.where(index % 2 == 0, own[None, None], chosen), PAIR, 0, 0)

    scores = [pltpu.VMEM((2 * PEERS, BLK, ROWS), f32)]
    weights, attended, upstream, inverse, part = call(
        forward_kernel,
        "forward",
        (shape((2 * PEERS, BLK, ROWS), bf16), columns, columns, row, shape((2, BLK), f32)),
        1, 4, scores, 550_000_000, 5_000_000,
    )(nearby_block_mask, queries, gathered, grad_out, gain)
    sums = lax.all_to_all(jnp.broadcast_to(part[None], (KV_HEADS, 2, BLK)), "head", 0, 0)
    terms, grad_t, normed_t = call(
        backward_kernel,
        "backward",
        (shape((PEERS, 2) + block, bf16), columns, columns),
        0, 7, (), 1_100_000_000, 5_000_000,
    )(queries, gathered, weights, attended, upstream, inverse, sums)
    returned = lax.all_to_all(terms, PAIR, 0, 0)
    half = shape(block, bf16)
    to_below, to_above = call(far_sums_kernel, "far_sums", (half, half), 0, 1, (), 1_000_000, 600_000)(returned)
    from_above = two_planes(to_below, -1)
    from_below = two_planes(to_above, 1)
    tall = shape((BLK, GROUP * DH), bf16)
    near_sum, grad_queries, normed_out = call(
        near_sums_kernel, "near_sums", (shape(block, f32), tall, tall), 0, 4, (), 1_000_000, 1_500_000
    )(returned, grad_t, normed_t, gain)
    piece = shape((BLK, DH), bf16)
    grad_keys, grad_values = call(last_kernel, "last", (piece, piece), 0, 3, (), 1_000_000, 300_000)(
        near_sum, from_above, from_below
    )
    return normed_out, grad_queries, grad_keys, grad_values


def solution(mesh):
    spans, heads = mesh.devices.shape
    fine = Mesh(mesh.devices.reshape(spans // 8, 2, 4, heads), ("zq", "zp", "y", "head"))
    seq = ("zq", "zp", "y")
    both = P(seq, "head")
    return jax.shard_map(
        per_device,
        mesh=fine,
        in_specs=(both, both, both, P("head"), both, P(seq, None)),
        out_specs=(both, both, both, both),
        check_vma=False,
    )
```

```python
import math

import jax
import jax.numpy as jnp
from jax import lax
from jax.experimental import pallas as pl
from jax.experimental.pallas import tpu as pltpu
from jax.sharding import Mesh
from jax.sharding import PartitionSpec as P

HEADS = 32
KV_HEADS = 8
GROUP = HEADS // KV_HEADS
DH = 128
BLK = 128
ROWS = GROUP * BLK
PEERS = 8
FORWARD_STEP = 2
BACKWARD_STEP = 4
NEGATIVE = -1e30
EPSILON = 1e-06
FEATURES = HEADS * DH
SCALING = DH ** (-0.5)
EXP2_SCALE = SCALING / math.log(2.0)
PAIR = ("zp", "y")
VMEM_LIMIT = 12 * 1024 * 1024


def window_slot(zp, y, peer, part):
    peer_zp, peer_y = peer // 4, peer % 4
    across = (zp - peer_zp) & 1
    shift = peer_y - y
    if part == 0:
        return 8 + shift + across * (4 * (1 - 2 * zp))
    same = shift & 15
    other = 8 + shift - 4 * (1 - 2 * zp)
    return jnp.where(across == 1, other, same)


def stacked(array):
    return jnp.concatenate([array[:, g * DH : (g + 1) * DH] for g in range(GROUP)], axis=0)


def stacked_t(array):
    return jnp.concatenate([array[:, g * DH : (g + 1) * DH].T for g in range(GROUP)], axis=1)


def unstacked_t(array):
    return jnp.concatenate([array[:, g * BLK : (g + 1) * BLK].T for g in range(GROUP)], axis=1)


def over_groups(row):
    return sum(row[:, g * BLK : (g + 1) * BLK] for g in range(GROUP))


def to_groups(row):
    return jnp.concatenate([row] * GROUP, axis=1)


def joined(ref, first, count, which):
    return jnp.concatenate([ref[slot // 2, slot % 2, which] for slot in range(first, first + count)], axis=0)


def forward_kernel(mask, q_ref, kv_ref, up_ref, gain_ref, w_ref, att_ref, up_out, inv_ref, part_ref, s_ref):
    zp, y = lax.axis_index("zp"), lax.axis_index("y")
    q_t = stacked_t(q_ref[...])
    top = jnp.full((8, ROWS), NEGATIVE, jnp.float32)
    for first in range(0, 2 * PEERS, FORWARD_STEP):
        raw = jnp.dot(joined(kv_ref, first, FORWARD_STEP, 0), q_t, preferred_element_type=jnp.float32)
        for step in range(FORWARD_STEP):
            slot = first + step
            bias = jnp.where(mask[0, window_slot(zp, y, slot // 2, slot % 2)] > 0, 0.0, NEGATIVE)
            block = raw[step * BLK : (step + 1) * BLK] + bias
            s_ref[slot] = block
            top = jnp.maximum(top, block.reshape(BLK // 8, 8, ROWS).max(axis=0))
    top = top.max(axis=0, keepdims=True)
    total = jnp.zeros((8, ROWS), jnp.float32)
    numer = jnp.zeros((DH, ROWS), jnp.float32)
    for first in range(0, 2 * PEERS, FORWARD_STEP):
        for slot in range(first, first + FORWARD_STEP):
            weights = jnp.exp2((s_ref[slot] - top) * EXP2_SCALE)
            total = total + weights.reshape(BLK // 8, 8, ROWS).sum(axis=0)
            w_ref[slot] = weights.astype(jnp.bfloat16)
        rounded = w_ref[first : first + FORWARD_STEP].reshape(FORWARD_STEP * BLK, ROWS)
        values_t = joined(kv_ref, first, FORWARD_STEP, 1).T
        numer = numer + jnp.dot(values_t, rounded, preferred_element_type=jnp.float32)
    inverse = 1.0 / total.sum(axis=0, keepdims=True)
    attended = numer * inverse
    att_ref[...] = attended
    inv_ref[...] = jnp.broadcast_to(inverse, (8, ROWS))
    upstream = stacked_t(up_ref[...].astype(jnp.float32) * gain_ref[...])
    up_out[...] = upstream
    squares = over_groups(jnp.sum(attended * attended, axis=0, keepdims=True))
    products = over_groups(jnp.sum(upstream * attended, axis=0, keepdims=True))
    part_ref[...] = jnp.concatenate([squares, products], axis=0)


def rows_of(do_t):
    return jnp.concatenate([do_t[:, g * BLK : (g + 1) * BLK].T for g in range(GROUP)], axis=0)


def backward_kernel(q_ref, kv_ref, w_ref, att_ref, up_ref, inv_ref, sums_ref, terms_ref, grad_ref, normed_ref):
    sums = sums_ref[0]
    for peer in range(1, KV_HEADS):
        sums = sums + sums_ref[peer]
    root = jnp.sqrt(sums[0:1] / FEATURES + EPSILON)
    inv_root = 1.0 / root
    inner = sums[1:2] * inv_root
    attended = att_ref[...]
    normed = attended * to_groups(inv_root)
    normed_ref[...] = normed
    d_att = (up_ref[...] - normed * to_groups(inner / FEATURES)) * to_groups(inv_root)
    d_att = d_att.astype(jnp.bfloat16).astype(jnp.float32)
    inverse = inv_ref[0:1]
    delta = jnp.sum(d_att * attended, axis=0, keepdims=True) * inverse
    do_t = (d_att * inverse).astype(jnp.bfloat16)
    do_rows = rows_of(do_t)
    q_rows = stacked(q_ref[...])
    grad = jnp.zeros((DH, ROWS), jnp.float32)
    for first in range(0, 2 * PEERS, BACKWARD_STEP):
        weights = w_ref[first : first + BACKWARD_STEP].reshape(BACKWARD_STEP * BLK, ROWS)
        d_prob = jnp.dot(joined(kv_ref, first, BACKWARD_STEP, 1), do_t, preferred_element_type=jnp.float32)
        d_score = (weights.astype(jnp.float32) * (d_prob - delta)).astype(jnp.bfloat16)
        term_k = (jnp.dot(d_score, q_rows, preferred_element_type=jnp.float32) * SCALING).astype(jnp.bfloat16)
        term_v = jnp.dot(weights, do_rows, preferred_element_type=jnp.float32).astype(jnp.bfloat16)
        for step in range(BACKWARD_STEP):
            slot = first + step
            terms_ref[slot // 2, slot % 2, 0] = term_k[step * BLK : (step + 1) * BLK]
            terms_ref[slot // 2, slot % 2, 1] = term_v[step * BLK : (step + 1) * BLK]
        keys_t = joined(kv_ref, first, BACKWARD_STEP, 0).T
        grad = grad + jnp.dot(keys_t, d_score, preferred_element_type=jnp.float32)
    grad_ref[...] = grad


def far_sums_kernel(terms_ref, below_ref, above_ref):
    zp, y = lax.axis_index("zp"), lax.axis_index("y")
    below = jnp.zeros((2, BLK, DH), jnp.float32)
    above = jnp.zeros((2, BLK, DH), jnp.float32)
    for peer in range(PEERS):
        take = jnp.where(zp == peer // 4, y >= peer % 4, zp == 1)
        share = jnp.where(take, 1.0, 0.0)
        term = terms_ref[peer, 1].astype(jnp.float32)
        below = below + term * share
        above = above + term * (1.0 - share)
    below_ref[...] = below.astype(jnp.bfloat16)
    above_ref[...] = above.astype(jnp.bfloat16)


def near_sums_kernel(terms_ref, grad_ref, normed_ref, gain_ref, sum_ref, grad_out, out_ref):
    total = jnp.zeros((2, BLK, DH), jnp.float32)
    for peer in range(PEERS):
        total = total + terms_ref[peer, 0].astype(jnp.float32)
    sum_ref[...] = total
    grad_out[...] = (unstacked_t(grad_ref[...]) * SCALING).astype(jnp.bfloat16)
    out_ref[...] = (unstacked_t(normed_ref[...]) * gain_ref[...]).astype(jnp.bfloat16)


def last_kernel(near_ref, above_ref, below_ref, keys_ref, values_ref):
    total = near_ref[...] + below_ref[...].astype(jnp.float32) + above_ref[...].astype(jnp.float32)
    keys_ref[...] = total[0].astype(jnp.bfloat16)
    values_ref[...] = total[1].astype(jnp.bfloat16)


def shape(dims, dtype):
    return jax.ShapeDtypeStruct(dims, dtype)


def in_vmem(count):
    return [pl.BlockSpec(memory_space=pltpu.VMEM)] * count


def in_smem(count):
    return [pl.BlockSpec(memory_space=pltpu.SMEM)] * count


def two_planes(array, by):
    length = lax.axis_size("zq")
    return lax.ppermute(array, "zq", [(i, i + by) for i in range(length) if 0 <= i + by < length])


def call(kernel, name, outs, smem, vmem, scratch=(), flops=0, size=0):
    specs = tuple(in_vmem(len(outs)))
    return pl.pallas_call(
        kernel,
        out_shape=tuple(outs),
        in_specs=in_smem(smem) + in_vmem(vmem),
        out_specs=specs,
        scratch_shapes=list(scratch),
        compiler_params=pltpu.CompilerParams(vmem_limit_bytes=VMEM_LIMIT),
        cost_estimate=pl.CostEstimate(flops=flops, bytes_accessed=size, transcendentals=0),
        name=name,
    )


def per_device(queries, keys_in, values_in, norm_gain, grad_out, nearby_block_mask):
    zp, y = lax.axis_index("zp"), lax.axis_index("y")
    gain = norm_gain.reshape(1, -1)
    bf16, f32 = jnp.bfloat16, jnp.float32
    block = (2, BLK, DH)
    columns = shape((DH, ROWS), f32)
    row = shape((8, ROWS), f32)

    own = jnp.stack([keys_in, values_in])
    above = two_planes(own, -1)
    below = two_planes(own, 1)
    index = jnp.arange(2 * PEERS, dtype=jnp.int32).reshape(PEERS, 2, 1, 1, 1)
    to_zp, to_y = index // 8, index // 2 % 4
    take_below = jnp.where(to_zp == zp, y >= to_y, zp == 1)
    chosen = jnp.where(take_below, below[None, None], above[None, None])
    gathered = lax.all_to_all(jnp.where(index % 2 == 0, own[None, None], chosen), PAIR, 0, 0)

    scores = [pltpu.VMEM((2 * PEERS, BLK, ROWS), f32)]
    weights, attended, upstream, inverse, part = call(
        forward_kernel,
        "forward",
        (shape((2 * PEERS, BLK, ROWS), bf16), columns, columns, row, shape((2, BLK), f32)),
        1, 4, scores, 550_000_000, 5_000_000,
    )(nearby_block_mask, queries, gathered, grad_out, gain)
    sums = lax.all_to_all(jnp.broadcast_to(part[None], (KV_HEADS, 2, BLK)), "head", 0, 0)
    terms, grad_t, normed_t = call(
        backward_kernel,
        "backward",
        (shape((PEERS, 2) + block, bf16), columns, columns),
        0, 7, (), 1_100_000_000, 5_000_000,
    )(queries, gathered, weights, attended, upstream, inverse, sums)
    returned = lax.all_to_all(terms, PAIR, 0, 0)
    half = shape(block, bf16)
    to_below, to_above = call(far_sums_kernel, "far_sums", (half, half), 0, 1, (), 1_000_000, 600_000)(returned)
    from_above = two_planes(to_below, -1)
    from_below = two_planes(to_above, 1)
    tall = shape((BLK, GROUP * DH), bf16)
    near_sum, grad_queries, normed_out = call(
        near_sums_kernel, "near_sums", (shape(block, f32), tall, tall), 0, 4, (), 1_000_000, 1_500_000
    )(returned, grad_t, normed_t, gain)
    piece = shape((BLK, DH), bf16)
    grad_keys, grad_values = call(last_kernel, "last", (piece, piece), 0, 3, (), 1_000_000, 300_000)(
        near_sum, from_above, from_below
    )
    return normed_out, grad_queries, grad_keys, grad_values


def solution(mesh):
    spans, heads = mesh.devices.shape
    fine = Mesh(mesh.devices.reshape(spans // 8, 2, 4, heads), ("zq", "zp", "y", "head"))
    seq = ("zq", "zp", "y")
    both = P(seq, "head")
    return jax.shard_map(
        per_device,
        mesh=fine,
        in_specs=(both, both, both, P("head"), both, P(seq, None)),
        out_specs=(both, both, both, both),
        check_vma=False,
    )
```
